1024 devices in a mesh: row: 32 (over z, y_lo), col: 32 (over x, y_hi, core).
Axes of the slice: x: 8, y: 8 (y_hi: 2, y_lo: 4; y = y_hi * 4 + y_lo), z: 8, core: 2. Of those that a mesh axis runs over, the one named last changes fastest.
Arguments:
- basis_vectors: float32 [8, 1048576], P(None, ('row', 'col')), may hold values from -6 to 6
- ham_tiles: float32 [32, 32, 1024, 256], P('row', 'col'), may hold values from -0.1875 to 0.1875
- tile_rows: int32 [32, 32, 4], P('row', 'col'), may hold values from 0 to 127
- tile_cols: int32 [32, 32, 4], P('row', 'col'), may hold values from 0 to 127
- tile_count: int32 [32, 32], P('row', 'col'), may hold values from 1 to 4, as said below
Outputs:
- applied: float32 [8, 1048576], P(None, ('row', 'col'))
The draws below stay inside these ranges and needn't reach their ends.
Inputs may be any that keep to these rules, and one draw needn't show every extreme that they name: tile_count reaches 4 on some device and 1 on another.
All inputs are finite; a program needn't handle non-finite values.
Results may differ from the reference program's by a relative error of at most 0.0003.
Values sent between devices are 32-bit elements; how exact they have to be, the bound alone decides.
A program may use at most 32 MiB of HBM per device.

```python
import jax
import jax.numpy as jnp
from jax import lax

B = 256
VECS = 8
Q = 1024
TILES_DEV = 4
N = 1048576
SEG_ROW = 32768
SEG_COL = 32768
N_ROW = 32
N_COL = 32


def draw_tile_count(key, part):
    key = jax.random.fold_in(key, 7)
    first_key, place_key, other_key = jax.random.split(key, 3)
    total = N_ROW * N_COL
    counts = jax.random.randint(first_key, (total,), TILES_DEV // 4, TILES_DEV + 1)
    top_place = jax.random.randint(place_key, (), 0, total)
    low_place = (top_place + 1 + jax.random.randint(other_key, (), 0, total - 1)) % total
    counts = counts.at[top_place].set(TILES_DEV)
    counts = counts.at[low_place].set(TILES_DEV // 4)
    return counts.reshape(N_ROW, N_COL).astype(jnp.int32)


def place_ends(drawn, stream_key, low, high):
    longest = drawn.shape.index(max(drawn.shape))
    spots = []
    for shift in (0, 1):
        where = [jax.random.randint(jax.random.fold_in(stream_key, axis), (), 0, length) for axis, length in enumerate(drawn.shape)]
        where[longest] = (where[longest] + shift) % drawn.shape[longest]
        spots.append(tuple(where))
    return drawn.at[spots[0]].set(low).at[spots[1]].set(high)


def shard_levels(own_key, extent, pieces, smallest, top_value):
    level = 1.0
    for axis_at, parts in pieces:
        draws = jax.random.uniform(jax.random.fold_in(jax.random.fold_in(own_key, 6), axis_at), (parts,), jnp.float32, smallest / len(pieces), top_value / len(pieces))
        level = level * jnp.repeat(jnp.exp(draws), extent[axis_at] // parts).reshape((-1,) + (1,) * (len(extent) - 1 - axis_at))
    return level


def scatter_about(stream_key, shape, scale, limit, cuts=(), kind=jnp.bfloat16):
    values = scale * jax.random.normal(stream_key, shape, jnp.float32)
    if cuts:
        values = values * shard_levels(stream_key, shape, cuts, -0.22, 0.18)
    return jnp.clip(values, -limit, limit).astype(kind)


def setup_inputs(seed: int = 0) -> dict:
    key_list = jax.random.split(jax.random.key(seed), 6)
    return {
        "basis_vectors": scatter_about(key_list[0], (VECS, N), 1.0, 6.0, ((1, 1024),), jnp.float32),
        "ham_tiles": scatter_about(key_list[1], (N_ROW, N_COL, TILES_DEV * B, B), (4 * B) ** -0.5, 0.1875, ((0, 32), (1, 32)), jnp.float32),
        "tile_rows": place_ends(jax.random.randint(key_list[2], (N_ROW, N_COL, TILES_DEV), 0, SEG_ROW // B), jax.random.fold_in(key_list[2], 1), 0, (SEG_ROW // B) - 1).astype(jnp.int32),
        "tile_cols": place_ends(jax.random.randint(key_list[3], (N_ROW, N_COL, TILES_DEV), 0, SEG_COL // B), jax.random.fold_in(key_list[3], 1), 0, (SEG_COL // B) - 1).astype(jnp.int32),
        "tile_count": draw_tile_count(jax.random.fold_in(key_list[5], 71), 0),
    }


def reference(basis_vectors, ham_tiles, tile_rows, tile_cols, tile_count):
    seg_row = Q * N_COL
    flat_tiles = ham_tiles.reshape(N_ROW * N_COL * TILES_DEV, B, B)
    row_tiles = tile_rows.reshape(-1)
    col_tiles = tile_cols.reshape(-1)
    counts = tile_count.reshape(-1)
    offsets = jnp.arange(B, dtype=jnp.int32)

    def step(result, flat_index):
        device = flat_index // TILES_DEV
        slot_index = flat_index % TILES_DEV
        dev_row = device // N_COL
        dev_col = device % N_COL
        is_live = (slot_index < counts[device]).astype(jnp.float32)
        one_tile = flat_tiles[flat_index] * is_live
        row_index = (dev_row * seg_row + row_tiles[flat_index] * B + offsets).astype(jnp.int32)
        local_col = col_tiles[flat_index] * B + offsets
        col_index = ((local_col // Q * N_COL + dev_col) * Q + local_col % Q).astype(jnp.int32)
        row_part = basis_vectors[:, row_index]
        col_part = basis_vectors[:, col_index]
        direct = jnp.dot(col_part, one_tile.T, precision=lax.Precision.HIGHEST, preferred_element_type=jnp.float32)
        mirror = jnp.dot(row_part, one_tile, precision=lax.Precision.HIGHEST, preferred_element_type=jnp.float32)
        result = result.at[:, row_index].add(direct)
        result = result.at[:, col_index].add(mirror)
        return result, None

    start = jnp.zeros(basis_vectors.shape, jnp.float32)
    applied, _ = lax.scan(step, start, jnp.arange(N_ROW * N_COL * TILES_DEV, dtype=jnp.int32))
    return applied
```

```python
import functools

import jax
import jax.numpy as jnp
from jax import lax
from jax.experimental import pallas as pl
from jax.experimental.pallas import tpu as pltpu
from jax.sharding import PartitionSpec as P

MESH = pl.DeviceIdType.MESH
AXES = ("col", "row")
SMALL = 4


def kernel(
    bigs,
    subs,
    vectors_hbm,
    tiles_hbm,
    rows_hbm,
    cols_hbm,
    count_hbm,
    out_ref,
    tiles,
    high,
    low,
    vectors,
    own,
    given_rows,
    given_cols,
    given_count,
    places,
    held_0,
    held_1,
    stage,
    picked_0,
    picked_1,
    products,
    marks,
    partial,
    arrived,
    ready,
    local_sem,
    place_send,
    place_recv,
    wide_send,
    wide_recv,
    pick_send,
    pick_recv,
    product_send,
    product_recv,
    sum_send,
    sum_recv,
):
    slots, width = tiles.shape[0], tiles.shape[1]
    small = SMALL
    given = (given_rows, given_cols)
    held, picked = (held_0, held_1), (picked_0, picked_1)
    me = [lax.axis_index(axis) for axis in AXES]
    my_big = [lax.div(m, small) for m in me]
    my_small = [lax.rem(m, small) for m in me]

    def each_big(a, act):
        @pl.loop(0, bigs[a])
        def _(rank):
            big = rank
            if a == 0:
                odd = lax.rem(rank, 2)
                half = lax.div(rank + 1, 2)
                big = odd * half + (1 - odd) * lax.rem(bigs[a] - half, bigs[a])

            @pl.when(big != my_big[a])
            def _():
                act(big)

    def each_small(a, act):
        @pl.loop(1, small)
        def _(step):
            act(lax.rem(my_small[a] + step, small))

    def at(a, big, little):
        return {AXES[a]: big * small + little}

    core = lax.rem(me[0], 2)
    first_core = core == 0
    barrier = pltpu.get_barrier_semaphore()

    def greet(**where):
        pl.semaphore_signal(barrier, inc=1, device_id=where, device_id_type=MESH)

    each_big(0, lambda big: greet(col=big * small + my_small[0] - core))

    @pl.loop(1, small // 2)
    def _(step):
        greet(col=my_big[0] * small + lax.rem(my_small[0] - core + 2 * step, small))

    @pl.when(core == 1)
    def _():
        greet(col=me[0] - 1)

    each_big(1, lambda big: greet(row=big * small + my_small[1], col=me[0] - core + 1))
    each_small(
        1, lambda little: greet(row=my_big[1] * small + little, col=me[0] - core + 1)
    )

    local = [
        pltpu.make_async_copy(source, target, local_sem.at[index])
        for index, (source, target) in enumerate(
            [
                (vectors_hbm, vectors),
                (rows_hbm, given_rows),
                (cols_hbm, given_cols),
                (count_hbm, given_count),
                (tiles_hbm, tiles),
            ]
        )
    ]
    for copy in local:
        copy.start()
    for copy in local[:-1]:
        copy.wait()

    for sub in range(subs):
        own[sub] = vectors[:, sub * width : (sub + 1) * width]
    for a in range(2):
        for slot in range(slots):
            place = given[a][0, 0, slot]
            places[a, my_small[a], slot] = place
            places[a, my_small[a], slots + slot] = lax.div(place, small * subs) * subs + lax.rem(
                place, subs
            )

    def complete(a):
        mine = first_core if a == 0 else core == 1
        count = 2 * (bigs[0] - 1) + small - 1 if a == 0 else 2 * (bigs[1] + small - 2)

        @pl.when(mine)
        def _():
            pl.semaphore_wait(barrier, count)
            pl.semaphore_signal(
                ready, inc=1, device_id={"col": me[0] + 1 - 2 * a}, device_id_type=MESH
            )

        @pl.when(jnp.logical_not(mine))
        def _():
            pl.semaphore_wait(ready, 1)

    def place_copy(a, little):
        mine = places.at[a, my_small[a]]
        return pltpu.make_async_remote_copy(
            src_ref=mine,
            dst_ref=mine,
            send_sem=place_send.at[a],
            recv_sem=place_recv.at[a],
            device_id=at(a, my_big[a], little),
            device_id_type=MESH,
        )

    def wide_copy(a, big):
        return pltpu.make_async_remote_copy(
            src_ref=own,
            dst_ref=held[a].at[pl.ds(my_big[a] * subs, subs)],
            send_sem=wide_send.at[a],
            recv_sem=wide_recv.at[a],
            device_id=at(a, big, my_small[a]),
            device_id_type=MESH,
        )

    for a in range(2):
        complete(a)
        each_big(a, lambda big: wide_copy(a, big).start())
        each_small(a, lambda little: place_copy(a, little).start())
    for a in range(2):
        for sub in range(subs):
            held[a][my_big[a] * subs + sub] = own[sub]

    local[-1].wait()
    for slot in range(slots):
        whole = tiles[slot]
        top = whole.astype(jnp.bfloat16)
        high[slot] = top
        low[slot] = (whole - top.astype(jnp.float32)).astype(jnp.bfloat16)

    def wait_all(buffer, count, sem):
        landed = buffer.at[pl.ds(0, count)]
        pltpu.make_async_copy(landed, landed, sem).wait()

    def pick_copy(a, step):
        return pltpu.make_async_remote_copy(
            src_ref=stage.at[a, step],
            dst_ref=picked[a].at[pl.ds(my_small[a] * slots, slots)],
            send_sem=pick_send.at[a],
            recv_sem=pick_recv.at[a],
            device_id=at(a, my_big[a], lax.rem(my_small[a] + step, small)),
            device_id_type=MESH,
        )

    def pick(a):
        wait_all(held[a], (bigs[a] - 1) * subs, wide_recv.at[a])
        for step in range(1, small):
            little = lax.rem(my_small[a] + step, small)
            for slot in range(slots):
                stage[a, step, slot] = held[a][places[a, little, slots + slot]]
            pick_copy(a, step).start()
        for slot in range(slots):
            picked[a][my_small[a] * slots + slot] = held[a][places[a, my_small[a], slots + slot]]

    def mark(a):
        for index in range(small * slots):
            marks[a, index] = jnp.full(
                marks.shape[2:], places[a, index // slots, index % slots], jnp.int32
            )

    def block(a, slot):
        place = given[a][0, 0, slot]
        return picked[a][lax.rem(lax.div(place, subs), small) * slots + slot]

    def multiply(value, slot, tile_dim):
        top = value.astype(jnp.bfloat16).astype(jnp.float32)
        both = jnp.concatenate([top, value - top], axis=0).astype(jnp.bfloat16)
        dims = (((1,), (tile_dim,)), ((), ()))
        result = lax.dot_general(both, high[slot], dims, preferred_element_type=jnp.float32)
        result += lax.dot_general(both, low[slot], dims, preferred_element_type=jnp.float32)
        return result[: value.shape[0]] + result[value.shape[0] :]

    def product_copy(a, little):
        mine = products.at[a, pl.ds(my_small[a] * slots, slots)]
        return pltpu.make_async_remote_copy(
            src_ref=mine,
            dst_ref=mine,
            send_sem=product_send.at[a],
            recv_sem=product_recv.at[a],
            device_id=at(a, my_big[a], little),
            device_id_type=MESH,
        )

    def apply_tiles(a):
        wait_all(picked[1 - a], (small - 1) * slots, pick_recv.at[1 - a])
        for slot in range(slots):
            is_live = (slot < given_count[0, 0]).astype(jnp.float32)
            products[a, my_small[a] * slots + slot] = is_live * multiply(block(1 - a, slot), slot, 1 - a)
        each_small(a, lambda little: product_copy(a, little).start())

    def sum_copy(a, big):
        return pltpu.make_async_remote_copy(
            src_ref=partial.at[a, big],
            dst_ref=arrived.at[a, my_big[a]],
            send_sem=sum_send.at[a],
            recv_sem=sum_recv.at[a],
            device_id=at(a, big, my_small[a]),
            device_id_type=MESH,
        )

    def sum_for(a, big, target, target_index):
        first = (big * small + my_small[a]) * subs
        totals = [jnp.zeros(products.shape[2:], jnp.float32) for _ in range(subs)]
        for index in range(small * slots):
            value = products[a, index]
            spread = jnp.concatenate([marks[a, index]] * (width // marks.shape[3]), axis=1)
            for sub in range(subs):
                totals[sub] += jnp.where(spread == first + sub, value, 0.0)
        for sub in range(subs):
            target[a, target_index, sub] = totals[sub]

    def send_sum(a, big):
        sum_for(a, big, partial, big)
        sum_copy(a, big).start()

    def sums(a):
        wait_all(products.at[a], (small - 1) * slots, product_recv.at[a])
        each_big(a, lambda big: send_sum(a, big))
        sum_for(a, my_big[a], arrived, my_big[a])

    for a in range(2):
        wait_all(places.at[a], small - 1, place_recv.at[a])
    pick(0)
    pick(1)
    mark(1)
    apply_tiles(1)
    mark(0)
    apply_tiles(0)
    sums(1)
    sums(0)

    totals = []
    for a in range(2):
        wait_all(arrived.at[a], bigs[a] - 1, sum_recv.at[a])
        for sub in range(subs):
            total = arrived[a, 0, sub]
            for big in range(1, bigs[a]):
                total += arrived[a, big, sub]
            totals.append(total)
    for sub in range(subs):
        out_ref[:, sub * width : (sub + 1) * width] = totals[sub] + totals[subs + sub]

    for a in range(2):
        wait_all(places.at[a], small - 1, place_send.at[a])
        wait_all(held[a], (bigs[a] - 1) * subs, wide_send.at[a])
        wait_all(stage.at[a], small - 1, pick_send.at[a])
        wait_all(products.at[a], (small - 1) * slots, product_send.at[a])
        wait_all(partial.at[a], bigs[a] - 1, sum_send.at[a])


def solution(mesh):
    bigs = tuple(mesh.shape[axis] // SMALL for axis in AXES)
    most = max(bigs)

    def per_device(basis_vectors, ham_tiles, tile_rows, tile_cols, tile_count):
        vecs, piece = basis_vectors.shape
        width = ham_tiles.shape[-1]
        slots = ham_tiles.shape[2] // width
        subs = piece // width
        block = (vecs, width)
        dma = pltpu.SemaphoreType.DMA
        place = pltpu.SMEM((1, 1, slots), jnp.int32)
        return pl.pallas_call(
            functools.partial(kernel, bigs, subs),
            out_shape=pltpu.VMEM((vecs, piece), jnp.float32),
            in_specs=[pl.BlockSpec(memory_space=pl.ANY)] * 5,
            out_specs=pl.BlockSpec(memory_space=pltpu.VMEM),
            scratch_shapes=[
                pltpu.VMEM((slots, width, width), jnp.float32),
                pltpu.VMEM((slots, width, width), jnp.bfloat16),
                pltpu.VMEM((slots, width, width), jnp.bfloat16),
                pltpu.VMEM((vecs, piece), jnp.float32),
                pltpu.VMEM((subs,) + block, jnp.float32),
                place,
                place,
                pltpu.SMEM((1, 1), jnp.int32),
                pltpu.SMEM((2, SMALL, 2 * slots), jnp.int32),
                pltpu.VMEM((bigs[0] * subs,) + block, jnp.float32),
                pltpu.VMEM((bigs[1] * subs,) + block, jnp.float32),
                pltpu.VMEM((2, SMALL, slots) + block, jnp.float32),
                pltpu.VMEM((SMALL * slots,) + block, jnp.float32),
                pltpu.VMEM((SMALL * slots,) + block, jnp.float32),
                pltpu.VMEM((2, SMALL * slots) + block, jnp.float32),
                pltpu.VMEM((2, SMALL * slots, 8, 128), jnp.int32),
                pltpu.VMEM((2, most, subs) + block, jnp.float32),
                pltpu.VMEM((2, most, subs) + block, jnp.float32),
                pltpu.SemaphoreType.REGULAR,
                dma((5,)),
            ]
            + [dma((2,))] * 10,
            compiler_params=pltpu.CompilerParams(collective_id=0, has_side_effects=True),
            name="apply_pairs",
        )(basis_vectors, ham_tiles.reshape(slots, width, width), tile_rows, tile_cols, tile_count)

    placed = (
        P(None, ("row", "col")),
        P("row", "col", None, None),
        P("row", "col", None),
        P("row", "col", None),
        P("row", "col"),
    )
    return jax.shard_map(
        per_device, mesh=mesh, in_specs=placed, out_specs=P(None, ("row", "col")), check_vma=False
    )
```

```python
import functools

import jax
import jax.numpy as jnp
from jax import lax
from jax.experimental import pallas as pl
from jax.experimental.pallas import tpu as pltpu
from jax.sharding import PartitionSpec as P

MESH = pl.DeviceIdType.MESH
AXES = ("col", "row")
SMALL = 4


def kernel(
    bigs,
    subs,
    vectors_hbm,
    tiles_hbm,
    rows_hbm,
    cols_hbm,
    count_hbm,
    out_ref,
    tiles,
    high,
    low,
    vectors,
    own,
    given_rows,
    given_cols,
    given_count,
    places,
    held_0,
    held_1,
    stage,
    picked_0,
    picked_1,
    products,
    marks,
    partial,
    arrived,
    ready,
    local_sem,
    place_send,
    place_recv,
    wide_send,
    wide_recv,
    pick_send,
    pick_recv,
    product_send,
    product_recv,
    sum_send,
    sum_recv,
):
    slots, width = tiles.shape[0], tiles.shape[1]
    small = SMALL
    given = (given_rows, given_cols)
    held, picked = (held_0, held_1), (picked_0, picked_1)
    me = [lax.axis_index(axis) for axis in AXES]
    my_big = [lax.div(m, small) for m in me]
    my_small = [lax.rem(m, small) for m in me]

    def each_big(a, act, farthest=False):
        @pl.loop(0, bigs[a])
        def _(rank):
            big = rank
            if a == 0:
                half = lax.div(rank + 1, 2)
                offset = (1 - 2 * lax.rem(rank, 2)) * half
                if farthest:
                    big = lax.rem(my_big[0] + bigs[0] // 2 + offset + bigs[0], bigs[0])
                else:
                    big = lax.rem(bigs[0] - offset, bigs[0])

            @pl.when(big != my_big[a])
            def _():
                act(big)

    def each_small(a, act):
        @pl.loop(1, small)
        def _(step):
            act(lax.rem(my_small[a] + step, small))

    def at(a, big, little):
        return {AXES[a]: big * small + little}

    core = lax.rem(me[0], 2)
    first_late = bigs[1] // 2
    late = my_big[1] >= first_late
    is_late = late.astype(jnp.int32)
    barrier = pltpu.get_barrier_semaphore()

    def greet(**where):
        pl.semaphore_signal(barrier, inc=1, device_id=where, device_id_type=MESH)

    def touches_late(big):
        return jnp.maximum((big >= first_late).astype(jnp.int32), is_late)

    each_big(0, lambda big: greet(col=big * small + my_small[0] - core))
    each_big(
        1, lambda big: greet(row=big * small + my_small[1], col=me[0] - core + touches_late(big))
    )

    @pl.loop(1, small // 2)
    def _(step):
        greet(col=my_big[0] * small + lax.rem(my_small[0] - core + 2 * step, small))

    each_small(1, lambda little: greet(row=my_big[1] * small + little, col=me[0] - core))
    greet(col=me[0] + 1 - 2 * core)
    together = (1 - is_late) * (first_late - 1)
    counts = (
        2 * (bigs[0] - 1) + (small - 2) + 2 * (small - 1) + 2 * together + 1,
        2 * (bigs[1] - 1 - together) + 1,
    )

    local = [
        pltpu.make_async_copy(source, target, local_sem.at[index])
        for index, (source, target) in enumerate(
            [
                (vectors_hbm, vectors),
                (rows_hbm, given_rows),
                (cols_hbm, given_cols),
                (count_hbm, given_count),
                (tiles_hbm, tiles),
            ]
        )
    ]
    for copy in local:
        copy.start()
    for copy in local[:-1]:
        copy.wait()

    for sub in range(subs):
        own[sub] = vectors[:, sub * width : (sub + 1) * width]
    for a in range(2):
        for slot in range(slots):
            place = given[a][0, 0, slot]
            places[a, my_small[a], slot] = place
            places[a, my_small[a], slots + slot] = lax.div(place, small * subs) * subs + lax.rem(
                place, subs
            )

    def complete(gate):
        @pl.when(core == gate)
        def _():
            pl.semaphore_wait(barrier, counts[gate])
            pl.semaphore_signal(
                ready, inc=1, device_id={"col": me[0] + 1 - 2 * gate}, device_id_type=MESH
            )

        @pl.when(core != gate)
        def _():
            pl.semaphore_wait(ready, 1)

    def place_copy(a, little):
        mine = places.at[a, my_small[a]]
        return pltpu.make_async_remote_copy(
            src_ref=mine,
            dst_ref=mine,
            send_sem=place_send.at[a],
            recv_sem=place_recv.at[a],
            device_id=at(a, my_big[a], little),
            device_id_type=MESH,
        )

    def wide_copy(a, big):
        return pltpu.make_async_remote_copy(
            src_ref=own,
            dst_ref=held[a].at[pl.ds(my_big[a] * subs, subs)],
            send_sem=wide_send.at[a],
            recv_sem=wide_recv.at[a],
            device_id=at(a, big, my_small[a]),
            device_id_type=MESH,
        )

    def spread(a, chosen):
        def one(big):
            @pl.when(chosen(big))
            def _():
                wide_copy(a, big).start()

        each_big(a, one, farthest=True)

    def spread_places():
        for a in range(2):
            each_small(a, lambda little: place_copy(a, little).start())

    for a in range(2):
        for sub in range(subs):
            held[a][my_big[a] * subs + sub] = own[sub]

    def split_tiles():
        local[-1].wait()
        for slot in range(slots):
            whole = tiles[slot]
            top = whole.astype(jnp.bfloat16)
            high[slot] = top
            low[slot] = (whole - top.astype(jnp.float32)).astype(jnp.bfloat16)

    def wait_all(buffer, count, sem):
        landed = buffer.at[pl.ds(0, count)]
        pltpu.make_async_copy(landed, landed, sem).wait()

    def pick_copy(a, step):
        return pltpu.make_async_remote_copy(
            src_ref=stage.at[a, step],
            dst_ref=picked[a].at[pl.ds(my_small[a] * slots, slots)],
            send_sem=pick_send.at[a],
            recv_sem=pick_recv.at[a],
            device_id=at(a, my_big[a], lax.rem(my_small[a] + step, small)),
            device_id_type=MESH,
        )

    def pick(a):
        wait_all(places.at[a], small - 1, place_recv.at[a])
        wait_all(held[a], (bigs[a] - 1) * subs, wide_recv.at[a])
        for step in range(1, small):
            little = lax.rem(my_small[a] + step, small)
            for slot in range(slots):
                stage[a, step, slot] = held[a][places[a, little, slots + slot]]
            pick_copy(a, step).start()
        for slot in range(slots):
            picked[a][my_small[a] * slots + slot] = held[a][places[a, my_small[a], slots + slot]]

    def mark(a):
        for index in range(small * slots):
            marks[a, index] = jnp.full(
                marks.shape[2:], places[a, index // slots, index % slots], jnp.int32
            )

    def block(a, slot):
        place = given[a][0, 0, slot]
        return picked[a][lax.rem(lax.div(place, subs), small) * slots + slot]

    def multiply(value, slot, tile_dim):
        top = value.astype(jnp.bfloat16).astype(jnp.float32)
        both = jnp.concatenate([top, value - top], axis=0).astype(jnp.bfloat16)
        dims = (((1,), (tile_dim,)), ((), ()))
        result = lax.dot_general(both, high[slot], dims, preferred_element_type=jnp.float32)
        result += lax.dot_general(both, low[slot], dims, preferred_element_type=jnp.float32)
        return result[: value.shape[0]] + result[value.shape[0] :]

    def product_copy(a, little):
        mine = products.at[a, pl.ds(my_small[a] * slots, slots)]
        return pltpu.make_async_remote_copy(
            src_ref=mine,
            dst_ref=mine,
            send_sem=product_send.at[a],
            recv_sem=product_recv.at[a],
            device_id=at(a, my_big[a], little),
            device_id_type=MESH,
        )

    def apply_tiles(a):
        wait_all(picked[1 - a], (small - 1) * slots, pick_recv.at[1 - a])
        for slot in range(slots):
            is_live = (slot < given_count[0, 0]).astype(jnp.float32)
            products[a, my_small[a] * slots + slot] = is_live * multiply(block(1 - a, slot), slot, 1 - a)
        each_small(a, lambda little: product_copy(a, little).start())

    def sum_copy(a, big):
        return pltpu.make_async_remote_copy(
            src_ref=partial.at[a, big],
            dst_ref=arrived.at[a, my_big[a]],
            send_sem=sum_send.at[a],
            recv_sem=sum_recv.at[a],
            device_id=at(a, big, my_small[a]),
            device_id_type=MESH,
        )

    def sum_for(a, big, target, target_index):
        first = (big * small + my_small[a]) * subs
        totals = [jnp.zeros(products.shape[2:], jnp.float32) for _ in range(subs)]
        for index in range(small * slots):
            value = products[a, index]
            spread = jnp.concatenate([marks[a, index]] * (width // marks.shape[3]), axis=1)
            for sub in range(subs):
                totals[sub] += jnp.where(spread == first + sub, value, 0.0)
        for sub in range(subs):
            target[a, target_index, sub] = totals[sub]

    def send_sum(a, big):
        sum_for(a, big, partial, big)
        sum_copy(a, big).start()

    def sums(a):
        wait_all(products.at[a], (small - 1) * slots, product_recv.at[a])
        each_big(a, lambda big: send_sum(a, big), farthest=True)
        sum_for(a, my_big[a], arrived, my_big[a])

    def start_first():
        complete(0)
        spread(1, lambda big: touches_late(big) == 0)
        spread(0, lambda big: big >= 0)
        spread_places()

    def start_second():
        complete(1)
        spread(1, lambda big: touches_late(big) == 1)

    @pl.when(late)
    def _():
        start_second()

    start_first()

    @pl.when(jnp.logical_not(late))
    def _():
        start_second()

    split_tiles()

    @pl.when(jnp.logical_not(late))
    def _():
        pick(0)
        pick(1)
        apply_tiles(0)
        apply_tiles(1)
        mark(0)
        sums(0)
        mark(1)
        sums(1)

    @pl.when(late)
    def _():
        pick(0)
        apply_tiles(1)
        pick(1)
        mark(1)
        sums(1)
        apply_tiles(0)
        mark(0)
        sums(0)

    totals = []
    for a in range(2):
        wait_all(arrived.at[a], bigs[a] - 1, sum_recv.at[a])
        for sub in range(subs):
            total = arrived[a, 0, sub]
            for big in range(1, bigs[a]):
                total += arrived[a, big, sub]
            totals.append(total)
    for sub in range(subs):
        out_ref[:, sub * width : (sub + 1) * width] = totals[sub] + totals[subs + sub]

    for a in range(2):
        wait_all(places.at[a], small - 1, place_send.at[a])
        wait_all(held[a], (bigs[a] - 1) * subs, wide_send.at[a])
        wait_all(stage.at[a], small - 1, pick_send.at[a])
        wait_all(products.at[a], (small - 1) * slots, product_send.at[a])
        wait_all(partial.at[a], bigs[a] - 1, sum_send.at[a])


def solution(mesh):
    bigs = tuple(mesh.shape[axis] // SMALL for axis in AXES)
    most = max(bigs)

    def per_device(basis_vectors, ham_tiles, tile_rows, tile_cols, tile_count):
        vecs, piece = basis_vectors.shape
        width = ham_tiles.shape[-1]
        slots = ham_tiles.shape[2] // width
        subs = piece // width
        block = (vecs, width)
        dma = pltpu.SemaphoreType.DMA
        place = pltpu.SMEM((1, 1, slots), jnp.int32)
        return pl.pallas_call(
            functools.partial(kernel, bigs, subs),
            out_shape=pltpu.VMEM((vecs, piece), jnp.float32),
            in_specs=[pl.BlockSpec(memory_space=pl.ANY)] * 5,
            out_specs=pl.BlockSpec(memory_space=pltpu.VMEM),
            scratch_shapes=[
                pltpu.VMEM((slots, width, width), jnp.float32),
                pltpu.VMEM((slots, width, width), jnp.bfloat16),
                pltpu.VMEM((slots, width, width), jnp.bfloat16),
                pltpu.VMEM((vecs, piece), jnp.float32),
                pltpu.VMEM((subs,) + block, jnp.float32),
                place,
                place,
                pltpu.SMEM((1, 1), jnp.int32),
                pltpu.SMEM((2, SMALL, 2 * slots), jnp.int32),
                pltpu.VMEM((bigs[0] * subs,) + block, jnp.float32),
                pltpu.VMEM((bigs[1] * subs,) + block, jnp.float32),
                pltpu.VMEM((2, SMALL, slots) + block, jnp.float32),
                pltpu.VMEM((SMALL * slots,) + block, jnp.float32),
                pltpu.VMEM((SMALL * slots,) + block, jnp.float32),
                pltpu.VMEM((2, SMALL * slots) + block, jnp.float32),
                pltpu.VMEM((2, SMALL * slots, 8, 128), jnp.int32),
                pltpu.VMEM((2, most, subs) + block, jnp.float32),
                pltpu.VMEM((2, most, subs) + block, jnp.float32),
                pltpu.SemaphoreType.REGULAR,
                dma((5,)),
            ]
            + [dma((2,))] * 10,
            compiler_params=pltpu.CompilerParams(collective_id=0, has_side_effects=True),
            name="apply_pairs",
        )(basis_vectors, ham_tiles.reshape(slots, width, width), tile_rows, tile_cols, tile_count)

    placed = (
        P(None, ("row", "col")),
        P("row", "col", None, None),
        P("row", "col", None),
        P("row", "col", None),
        P("row", "col"),
    )
    return jax.shard_map(
        per_device, mesh=mesh, in_specs=placed, out_specs=P(None, ("row", "col")), check_vma=False
    )
```

```python
import functools

import jax
import jax.numpy as jnp
from jax import lax
from jax.experimental import pallas as pl
from jax.experimental.pallas import tpu as pltpu
from jax.sharding import PartitionSpec as P

MESH = pl.DeviceIdType.MESH
AXES = ("col", "row")
SMALL = 4


def kernel(
    bigs,
    subs,
    vectors_hbm,
    tiles_hbm,
    rows_hbm,
    cols_hbm,
    count_hbm,
    out_ref,
    tiles,
    high,
    low,
    vectors,
    own,
    given_rows,
    given_cols,
    given_count,
    places,
    held_0,
    held_1,
    stage,
    picked_0,
    picked_1,
    products,
    marks,
    partial,
    arrived,
    ready,
    local_sem,
    place_send,
    place_recv,
    wide_send,
    wide_recv,
    pick_send,
    pick_recv,
    product_send,
    product_recv,
    sum_send,
    sum_recv,
):
    slots, width = tiles.shape[0], tiles.shape[1]
    small = SMALL
    given = (given_rows, given_cols)
    held, picked = (held_0, held_1), (picked_0, picked_1)
    me = [lax.axis_index(axis) for axis in AXES]
    my_big = [lax.div(m, small) for m in me]
    my_small = [lax.rem(m, small) for m in me]

    def each_big(a, act, farthest=False):
        @pl.loop(0, bigs[a])
        def _(rank):
            big = rank
            if a == 0:
                half = lax.div(rank + 1, 2)
                offset = (1 - 2 * lax.rem(rank, 2)) * half
                if farthest:
                    big = lax.rem(my_big[0] + bigs[0] // 2 + offset + bigs[0], bigs[0])
                else:
                    big = lax.rem(bigs[0] - offset, bigs[0])

            @pl.when(big != my_big[a])
            def _():
                act(big)

    steps = range(small - 1, 0, -1)

    def beside(a, step):
        if step == 1:
            return my_small[a] + 1 - 2 * lax.rem(my_small[a], 2)
        return lax.rem(my_small[a] + 2, 4) if step == 2 else 3 - my_small[a]

    def each_small(a, act):
        for step in steps:
            act(beside(a, step))

    def at(a, big, little):
        return {AXES[a]: big * small + little}

    core = lax.rem(me[0], 2)
    first_late = bigs[1] // 2
    late = my_big[1] >= first_late
    is_late = late.astype(jnp.int32)
    barrier = pltpu.get_barrier_semaphore()

    def greet(**where):
        pl.semaphore_signal(barrier, inc=1, device_id=where, device_id_type=MESH)

    def touches_late(big):
        return jnp.maximum((big >= first_late).astype(jnp.int32), is_late)

    each_big(0, lambda big: greet(col=big * small + my_small[0] - core))
    @pl.loop(1, small // 2)
    def _(step):
        greet(col=my_big[0] * small + lax.rem(my_small[0] - core + 2 * step, small))

    each_small(1, lambda little: greet(row=my_big[1] * small + little, col=me[0] - core))
    greet(col=me[0] + 1 - 2 * core)
    each_big(
        1, lambda big: greet(row=big * small + my_small[1], col=me[0] - core + touches_late(big))
    )
    together = (1 - is_late) * (first_late - 1)
    counts = (
        2 * (bigs[0] - 1) + (small - 2) + 2 * (small - 1) + 2 * together + 1,
        2 * (bigs[1] - 1 - together) + 1,
    )

    local = [
        pltpu.make_async_copy(source, target, local_sem.at[index])
        for index, (source, target) in enumerate(
            [
                (vectors_hbm, vectors),
                (rows_hbm, given_rows),
                (cols_hbm, given_cols),
                (count_hbm, given_count),
                (tiles_hbm, tiles),
            ]
        )
    ]
    for copy in local:
        copy.start()
    for copy in local[:-1]:
        copy.wait()

    for sub in range(subs):
        own[sub] = vectors[:, sub * width : (sub + 1) * width]
    for a in range(2):
        for slot in range(slots):
            place = given[a][0, 0, slot]
            places[a, my_small[a], slot] = place
            places[a, my_small[a], slots + slot] = lax.div(place, small * subs) * subs + lax.rem(
                place, subs
            )

    def complete(gate):
        @pl.when(core == gate)
        def _():
            pl.semaphore_wait(barrier, counts[gate])
            pl.semaphore_signal(
                ready, inc=1, device_id={"col": me[0] + 1 - 2 * gate}, device_id_type=MESH
            )

        @pl.when(core != gate)
        def _():
            pl.semaphore_wait(ready, 1)

    def place_copy(a, little):
        mine = places.at[a, my_small[a]]
        return pltpu.make_async_remote_copy(
            src_ref=mine,
            dst_ref=mine,
            send_sem=place_send.at[a],
            recv_sem=place_recv.at[a],
            device_id=at(a, my_big[a], little),
            device_id_type=MESH,
        )

    def wide_copy(a, big):
        return pltpu.make_async_remote_copy(
            src_ref=own,
            dst_ref=held[a].at[pl.ds(my_big[a] * subs, subs)],
            send_sem=wide_send.at[a],
            recv_sem=wide_recv.at[a],
            device_id=at(a, big, my_small[a]),
            device_id_type=MESH,
        )

    def spread(a, chosen):
        def one(big):
            @pl.when(chosen(big))
            def _():
                wide_copy(a, big).start()

        each_big(a, one, farthest=True)

    def spread_places():
        for a in range(2):
            each_small(a, lambda little: place_copy(a, little).start())

    for a in range(2):
        for sub in range(subs):
            held[a][my_big[a] * subs + sub] = own[sub]

    def split_tiles():
        local[-1].wait()
        for slot in range(slots):
            whole = tiles[slot]
            top = whole.astype(jnp.bfloat16)
            high[slot] = top
            low[slot] = (whole - top.astype(jnp.float32)).astype(jnp.bfloat16)

    def wait_all(buffer, count, sem):
        landed = buffer.at[pl.ds(0, count)]
        pltpu.make_async_copy(landed, landed, sem).wait()

    def pick_copy(a, step):
        return pltpu.make_async_remote_copy(
            src_ref=stage.at[a, step],
            dst_ref=picked[a].at[pl.ds(my_small[a] * slots, slots)],
            send_sem=pick_send.at[a],
            recv_sem=pick_recv.at[a],
            device_id=at(a, my_big[a], beside(a, step)),
            device_id_type=MESH,
        )

    def pick(a):
        wait_all(places.at[a], small - 1, place_recv.at[a])
        wait_all(held[a], (bigs[a] - 1) * subs, wide_recv.at[a])
        for step in steps:
            little = beside(a, step)
            for slot in range(slots):
                stage[a, step, slot] = held[a][places[a, little, slots + slot]]
            pick_copy(a, step).start()
        for slot in range(slots):
            picked[a][my_small[a] * slots + slot] = held[a][places[a, my_small[a], slots + slot]]

    def mark(a):
        for index in range(small * slots):
            marks[a, index] = jnp.full(
                marks.shape[2:], places[a, index // slots, index % slots], jnp.int32
            )

    def block(a, slot):
        place = given[a][0, 0, slot]
        return picked[a][lax.rem(lax.div(place, subs), small) * slots + slot]

    def multiply(value, slot, tile_dim):
        top = value.astype(jnp.bfloat16).astype(jnp.float32)
        both = jnp.concatenate([top, value - top], axis=0).astype(jnp.bfloat16)
        dims = (((1,), (tile_dim,)), ((), ()))
        result = lax.dot_general(both, high[slot], dims, preferred_element_type=jnp.float32)
        result += lax.dot_general(both, low[slot], dims, preferred_element_type=jnp.float32)
        return result[: value.shape[0]] + result[value.shape[0] :]

    def product_copy(a, little):
        mine = products.at[a, pl.ds(my_small[a] * slots, slots)]
        return pltpu.make_async_remote_copy(
            src_ref=mine,
            dst_ref=mine,
            send_sem=product_send.at[a],
            recv_sem=product_recv.at[a],
            device_id=at(a, my_big[a], little),
            device_id_type=MESH,
        )

    def apply_tiles(a):
        wait_all(picked[1 - a], (small - 1) * slots, pick_recv.at[1 - a])
        for slot in range(slots):
            is_live = (slot < given_count[0, 0]).astype(jnp.float32)
            products[a, my_small[a] * slots + slot] = is_live * multiply(block(1 - a, slot), slot, 1 - a)
        each_small(a, lambda little: product_copy(a, little).start())

    def sum_copy(a, big):
        return pltpu.make_async_remote_copy(
            src_ref=partial.at[a, big],
            dst_ref=arrived.at[a, my_big[a]],
            send_sem=sum_send.at[a],
            recv_sem=sum_recv.at[a],
            device_id=at(a, big, my_small[a]),
            device_id_type=MESH,
        )

    def sum_for(a, big, target, target_index):
        first = (big * small + my_small[a]) * subs
        totals = [jnp.zeros(products.shape[2:], jnp.float32) for _ in range(subs)]
        for index in range(small * slots):
            value = products[a, index]
            spread = jnp.concatenate([marks[a, index]] * (width // marks.shape[3]), axis=1)
            for sub in range(subs):
                totals[sub] += jnp.where(spread == first + sub, value, 0.0)
        for sub in range(subs):
            target[a, target_index, sub] = totals[sub]

    def send_sum(a, big):
        sum_for(a, big, partial, big)
        sum_copy(a, big).start()

    def sums(a):
        wait_all(products.at[a], (small - 1) * slots, product_recv.at[a])
        each_big(a, lambda big: send_sum(a, big))
        sum_for(a, my_big[a], arrived, my_big[a])

    def start_first():
        complete(0)
        spread(1, lambda big: touches_late(big) == 0)
        spread(0, lambda big: big >= 0)
        spread_places()

    def start_second():
        complete(1)
        spread(1, lambda big: touches_late(big) == 1)

    @pl.when(late)
    def _():
        start_second()

    start_first()

    @pl.when(jnp.logical_not(late))
    def _():
        start_second()

    split_tiles()

    @pl.when(jnp.logical_not(late))
    def _():
        pick(0)
        pick(1)
        apply_tiles(0)
        apply_tiles(1)
        mark(0)
        sums(0)
        mark(1)
        sums(1)

    @pl.when(late)
    def _():
        pick(0)
        pick(1)
        apply_tiles(1)
        mark(1)
        sums(1)
        apply_tiles(0)
        mark(0)
        sums(0)

    totals = []
    for a in range(2):
        wait_all(arrived.at[a], bigs[a] - 1, sum_recv.at[a])
        for sub in range(subs):
            total = arrived[a, 0, sub]
            for big in range(1, bigs[a]):
                total += arrived[a, big, sub]
            totals.append(total)
    for sub in range(subs):
        out_ref[:, sub * width : (sub + 1) * width] = totals[sub] + totals[subs + sub]

    for a in range(2):
        wait_all(places.at[a], small - 1, place_send.at[a])
        wait_all(held[a], (bigs[a] - 1) * subs, wide_send.at[a])
        wait_all(stage.at[a], small - 1, pick_send.at[a])
        wait_all(products.at[a], (small - 1) * slots, product_send.at[a])
        wait_all(partial.at[a], bigs[a] - 1, sum_send.at[a])


def solution(mesh):
    bigs = tuple(mesh.shape[axis] // SMALL for axis in AXES)
    most = max(bigs)

    def per_device(basis_vectors, ham_tiles, tile_rows, tile_cols, tile_count):
        vecs, piece = basis_vectors.shape
        width = ham_tiles.shape[-1]
        slots = ham_tiles.shape[2] // width
        subs = piece // width
        block = (vecs, width)
        dma = pltpu.SemaphoreType.DMA
        place = pltpu.SMEM((1, 1, slots), jnp.int32)
        return pl.pallas_call(
            functools.partial(kernel, bigs, subs),
            out_shape=pltpu.VMEM((vecs, piece), jnp.float32),
            in_specs=[pl.BlockSpec(memory_space=pl.ANY)] * 5,
            out_specs=pl.BlockSpec(memory_space=pltpu.VMEM),
            scratch_shapes=[
                pltpu.VMEM((slots, width, width), jnp.float32),
                pltpu.VMEM((slots, width, width), jnp.bfloat16),
                pltpu.VMEM((slots, width, width), jnp.bfloat16),
                pltpu.VMEM((vecs, piece), jnp.float32),
                pltpu.VMEM((subs,) + block, jnp.float32),
                place,
                place,
                pltpu.SMEM((1, 1), jnp.int32),
                pltpu.SMEM((2, SMALL, 2 * slots), jnp.int32),
                pltpu.VMEM((bigs[0] * subs,) + block, jnp.float32),
                pltpu.VMEM((bigs[1] * subs,) + block, jnp.float32),
                pltpu.VMEM((2, SMALL, slots) + block, jnp.float32),
                pltpu.VMEM((SMALL * slots,) + block, jnp.float32),
                pltpu.VMEM((SMALL * slots,) + block, jnp.float32),
                pltpu.VMEM((2, SMALL * slots) + block, jnp.float32),
                pltpu.VMEM((2, SMALL * slots, 8, 128), jnp.int32),
                pltpu.VMEM((2, most, subs) + block, jnp.float32),
                pltpu.VMEM((2, most, subs) + block, jnp.float32),
                pltpu.SemaphoreType.REGULAR,
                dma((5,)),
            ]
            + [dma((2,))] * 10,
            compiler_params=pltpu.CompilerParams(collective_id=0, has_side_effects=True),
            name="apply_pairs",
        )(basis_vectors, ham_tiles.reshape(slots, width, width), tile_rows, tile_cols, tile_count)

    placed = (
        P(None, ("row", "col")),
        P("row", "col", None, None),
        P("row", "col", None),
        P("row", "col", None),
        P("row", "col"),
    )
    return jax.shard_map(
        per_device, mesh=mesh, in_specs=placed, out_specs=P(None, ("row", "col")), check_vma=False
    )
```
